32 devices in a mesh: dp: 8 (over z, x), shard: 4 (over y, core).
Axes of the slice: x: 2, y: 2, z: 4, core: 2. Of those that a mesh axis runs over, the one named last changes fastest.
Arguments:
- gradient: bfloat16 [8, 2560, 2560], P(None, ('shard', 'dp')), may hold values from -1.5 to 1.5
- owner: int32 [8], replicated, may hold values from 0 to 7, each once
- a_inverse: bfloat16 [8, 2560, 2560], P('dp', 'shard'), as said below
- b_inverse: bfloat16 [8, 2560, 2560], P('dp', 'shard'), as said below
Outputs:
- preconditioned: bfloat16 [8, 2560, 2560], P(None, ('shard', 'dp'))
The draws below stay inside these ranges and needn't reach their ends.
Inputs may be any that keep to these rules, and one draw needn't show every extreme that they name: owner names each of the 8 slots for exactly one layer. Every slot of a_inverse is a symmetric matrix. Every slot of b_inverse is a symmetric matrix.
All inputs are finite; a program needn't handle non-finite values.
Results may differ from the reference program's by a relative error of at most 0.0049.
Values may be sent and summed in bfloat16 or wider, within the bound.
A program may use at most 128 MiB of HBM per device.

```python
import math
import jax
import jax.numpy as jnp
from jax import lax

DIM = 2560
LAYERS = 8


def factor_draw(key):
    first_key, second_key = jax.random.split(key, 2)
    noise = jax.random.normal(first_key, (LAYERS, DIM, DIM), jnp.float32)
    diagonal = jnp.exp(jax.random.uniform(second_key, (LAYERS, DIM), jnp.float32, math.log(1.5), math.log(4.0)))
    symmetric = (noise + jnp.swapaxes(noise, 1, 2)) * (0.6 / math.sqrt(2.0 * DIM))
    identity = jnp.eye(DIM, dtype=jnp.float32)
    return (symmetric + identity[None, :, :] * diagonal[:, None, :]).astype(jnp.bfloat16)


def draw_a_inverse(key, part):
    return factor_draw(jax.random.fold_in(key, 11))


def draw_b_inverse(key, part):
    return factor_draw(jax.random.fold_in(key, 23))


def steps_of(rng, extent, cuts, low, largest):
    factor_of = 1.0
    for dim, parts in cuts:
        heights = jax.random.uniform(jax.random.fold_in(jax.random.fold_in(rng, 6), dim), (parts,), jnp.float32, low / len(cuts), largest / len(cuts))
        factor_of = factor_of * jnp.repeat(jnp.exp(heights), extent[dim] // parts).reshape((-1,) + (1,) * (len(extent) - 1 - dim))
    return factor_of


def scatter_about(own_key, extent, deviation, bound, pieces=(), kind=jnp.bfloat16):
    drawn = deviation * jax.random.normal(own_key, extent, jnp.float32)
    if pieces:
        drawn = drawn * steps_of(own_key, extent, pieces, -0.22, 0.18)
    return jnp.clip(drawn, -bound, bound).astype(kind)


def setup_inputs(seed: int = 0) -> dict:
    key_list = jax.random.split(jax.random.key(seed), 5)
    return {
        "gradient": scatter_about(key_list[0], (LAYERS, DIM, DIM), 0.25, 1.5, ((1, 32),)),
        "owner": jax.random.permutation(key_list[1], LAYERS).astype(jnp.int32),
        "a_inverse": draw_a_inverse(jax.random.fold_in(key_list[4], 71), 0),
        "b_inverse": draw_b_inverse(jax.random.fold_in(key_list[4], 71), 0),
    }


def reference(gradient, owner, a_inverse, b_inverse):
    def one_layer(layer_index):
        holder = owner[layer_index]
        right_half = jnp.dot(gradient[layer_index], b_inverse[holder], preferred_element_type=jnp.float32).astype(jnp.bfloat16)
        return jnp.dot(a_inverse[holder], right_half, preferred_element_type=jnp.float32).astype(jnp.bfloat16)

    return lax.map(one_layer, jnp.arange(LAYERS, dtype=jnp.int32))
```

```python
import functools
import jax
import jax.numpy as jnp
from jax import lax
from jax.experimental import pallas as pl
from jax.experimental.pallas import tpu as pltpu
from jax.sharding import PartitionSpec as P

MESH = pl.DeviceIdType.MESH
F32 = jnp.float32
BF16 = jnp.bfloat16


def general(gradient, owner, a_inverse, b_inverse):
    layer_count = gradient.shape[0]
    chosen = (owner[:, None] == jnp.arange(layer_count, dtype=jnp.int32)[None, :]).astype(BF16)
    outgoing = jnp.einsum("lo,lrc->orc", chosen, gradient, preferred_element_type=F32).astype(BF16)
    owned = lax.all_to_all(outgoing, "dp", split_axis=0, concat_axis=1, tiled=True)
    right_half = jnp.dot(
        owned[0],
        lax.all_gather(b_inverse[0], "shard", axis=0, tiled=True),
        preferred_element_type=F32,
    ).astype(BF16)
    result_rows = jnp.dot(
        a_inverse[0],
        lax.all_gather(right_half, "shard", axis=0, tiled=True),
        preferred_element_type=F32,
    ).astype(BF16)
    returned = lax.all_to_all(
        result_rows[None, :, :], "dp", split_axis=1, concat_axis=0, tiled=True
    )
    return jnp.take(returned, owner, axis=0)


def copy_block(owner_ref, in_ref, out_ref):
    out_ref[...] = in_ref[...]


def permute(owner, array, scatter):
    layers, rows, dim = array.shape
    plain = lambda l, owner_ref: (l, 0, 0)
    moved = lambda l, owner_ref: (owner_ref[l], 0, 0)
    return pl.pallas_call(
        copy_block,
        out_shape=jax.ShapeDtypeStruct(array.shape, array.dtype),
        grid_spec=pltpu.PrefetchScalarGridSpec(
            num_scalar_prefetch=1,
            grid=(layers,),
            in_specs=[pl.BlockSpec((1, rows, dim), plain if scatter else moved)],
            out_specs=pl.BlockSpec((1, rows, dim), moved if scatter else plain),
        ),
        cost_estimate=pl.CostEstimate(flops=0, bytes_accessed=4 * layers * rows * dim, transcendentals=0),
    )(owner, array)


def flip(index, mask):
    total, place = 0, 1
    while place <= mask:
        bit = lax.rem(index // place, 2)
        total = total + (1 - 2 * bit) * place if mask & place else total
        place *= 2
    return index + total


def dot(left, right):
    return jnp.dot(left, right, preferred_element_type=F32)


def kernel(
    groups, width, tile, side,
    g_ref, a_ref, b_ref, o_ref,
    gbuf, bfull, abuf, asib, ap, rbuf, psend, prec, obuf,
    local_sem, g_send, g_recv, b_send, b_recv, r_send, r_recv, p_send, p_recv, o_send, o_recv,
):
    _, rows, dim = g_ref.shape
    quarter, half = dim // 4, dim // 2
    d = lax.axis_index("dp")
    s = lax.axis_index("shard")
    y, c = s // 2, lax.rem(s, 2)
    sib = 2 * y + 1 - c
    across = 2 * (1 - y) + c
    across_sib = 2 * (1 - y) + 1 - c

    def rows_of(index, size, count=None):
        return pl.ds(pl.multiple_of(index * size, size), count or size)

    def remote(src, dst, send, recv, device):
        return pltpu.make_async_remote_copy(
            src_ref=src, dst_ref=dst, send_sem=send, recv_sem=recv, device_id=device, device_id_type=MESH
        )

    barrier = pltpu.get_barrier_semaphore()
    for k in range(1, groups):
        pl.semaphore_signal(barrier, inc=1, device_id=(flip(d, k), s), device_id_type=MESH)
    for other in (sib, across):
        pl.semaphore_signal(barrier, inc=1, device_id=(d, other), device_id_type=MESH)
    pl.semaphore_wait(barrier, groups + 1)

    g_copies = {}
    for k in (4, 5, 6, 7, 2, 3, 1):
        peer = flip(d, k)
        g_copies[k] = remote(
            g_ref.at[peer], gbuf.at[rows_of(d, rows)], g_send.at[k], g_recv.at[k], (peer, s)
        )
        g_copies[k].start()
    own_half = rows_of(y, half)
    other_half = rows_of(1 - y, half)
    b_across = remote(
        b_ref.at[:, own_half], bfull.at[rows_of(s, quarter), own_half], b_send.at[0], b_recv.at[0], (d, across)
    )
    b_across.start()
    b_sib = remote(b_ref, bfull.at[rows_of(s, quarter)], b_send.at[1], b_recv.at[1], (d, sib))
    b_sib.start()
    a_sib = remote(a_ref.at[:, rows_of(across_sib, quarter)], asib, b_send.at[2], b_recv.at[2], (d, sib))
    a_sib.start()
    a_own = pltpu.make_async_copy(a_ref, abuf, local_sem.at[0])
    a_own.start()
    b_own = pltpu.make_async_copy(b_ref, bfull.at[rows_of(s, quarter)], local_sem.at[1])
    b_own.start()
    g_own = pltpu.make_async_copy(g_ref.at[d], gbuf.at[rows_of(d, rows)], local_sem.at[2])
    g_own.start()

    a_own.wait()
    per = quarter // side

    def turn_own(i, carry):
        u, v = i // per, lax.rem(i, per)
        block = abuf[rows_of(u, side), pl.ds(pl.multiple_of(across * quarter + v * side, side), side)]
        ap[rows_of(v, side), pl.ds(pl.multiple_of(c * quarter + u * side, side), side)] = block.T
        return carry

    lax.fori_loop(0, per * per, turn_own, 0)
    a_sib.wait_recv()

    def turn_sib(i, carry):
        u, v = i // per, lax.rem(i, per)
        block = asib[rows_of(u, side), rows_of(v, side)]
        ap[rows_of(v, side), pl.ds(pl.multiple_of((1 - c) * quarter + u * side, side), side)] = block.T
        return carry

    lax.fori_loop(0, per * per, turn_sib, 0)

    b_own.wait()
    b_sib.wait_recv()
    wide = half // side

    def turn_b(i, carry):
        u, v = i // wide, lax.rem(i, wide)
        block = bfull[
            pl.ds(pl.multiple_of(y * half + u * side, side), side),
            pl.ds(pl.multiple_of((1 - y) * half + v * side, side), side),
        ]
        bfull[
            pl.ds(pl.multiple_of((1 - y) * half + v * side, side), side),
            pl.ds(pl.multiple_of(y * half + u * side, side), side),
        ] = block.T
        return carry

    lax.fori_loop(0, wide * wide, turn_b, 0)

    arrived = bfull.at[rows_of(across, quarter), other_half]
    remote(arrived, arrived, b_send.at[0], b_recv.at[0], (d, across)).wait_recv()
    relay = remote(arrived, arrived, b_send.at[3], b_recv.at[3], (d, sib))
    relay.start()
    relay.wait_recv()

    pair = 2 * rows
    r_copies = []
    for step in range(groups // 2):
        first = flip(d // 2, step)
        if step == 0:
            g_own.wait()
            g_copies[1].wait_recv()
        else:
            g_copies[2 * step].wait_recv()
            g_copies[2 * step + 1].wait_recv()
        here = pl.ds(pl.multiple_of(c * quarter + first * pair, pair), pair)

        def product(t, carry, first=first, here=here):
            columns = rows_of(t, tile)
            rbuf[here, columns] = dot(gbuf[rows_of(first, pair), :], bfull[:, columns]).astype(BF16)
            return carry

        lax.fori_loop(0, dim // tile, product, 0)
        copy = remote(rbuf.at[here], rbuf.at[here], r_send.at[step], r_recv.at[step], (d, sib))
        copy.start()
        r_copies.append(copy)
    for copy in r_copies:
        copy.wait_recv()

    chunks = dim // width

    def give(j, carry):
        psend[j] = dot(ap[...], rbuf[:, rows_of(j, width)]).astype(BF16)
        remote(psend.at[j], prec.at[j], p_send.at[j], p_recv.at[j], (d, across)).start()
        return carry

    lax.fori_loop(0, chunks, give, 0)

    def finish(j, carry):
        columns = rows_of(j, width)
        mine = dot(abuf[:, own_half], rbuf[:, columns])
        remote(psend.at[j], prec.at[j], p_send.at[j], p_recv.at[j], (d, across)).wait_recv()
        obuf[:, columns] = (mine + prec[j].astype(F32)).astype(BF16)
        for k in (4, 5, 6, 7, 2, 3, 1):
            peer = flip(d, k)
            remote(
                obuf.at[rows_of(peer, rows), columns], o_ref.at[d, :, columns],
                o_send.at[k], o_recv.at[k], (peer, s),
            ).start()
        return carry

    lax.fori_loop(0, chunks, finish, 0)
    o_own = pltpu.make_async_copy(obuf.at[rows_of(d, rows)], o_ref.at[d], local_sem.at[3])
    o_own.start()

    for k in range(1, groups):
        g_copies[k].wait_send()
    for copy in (b_across, b_sib, a_sib, relay, *r_copies):
        copy.wait_send()

    def sent(j, carry):
        remote(psend.at[j], prec.at[j], p_send.at[j], p_recv.at[j], (d, across)).wait_send()
        return carry

    lax.fori_loop(0, chunks, sent, 0)
    o_own.wait()
    for k in range(1, groups):
        peer = flip(d, k)
        whole = remote(obuf.at[rows_of(peer, rows)], o_ref.at[peer], o_send.at[k], o_recv.at[k], (peer, s))
        whole.wait_send()
        whole.wait_recv()


def fused(gradient, owner, a_inverse, b_inverse):
    groups, rows, dim = gradient.shape
    quarter, half = dim // 4, dim // 2
    width, tile, side = 256, 512, 128
    chunks = dim // width
    outgoing = permute(owner, gradient, True)
    anywhere = pl.BlockSpec(memory_space=pl.ANY)
    dma = pltpu.SemaphoreType.DMA
    returned = pl.pallas_call(
        functools.partial(kernel, groups, width, tile, side),
        out_shape=jax.ShapeDtypeStruct(gradient.shape, BF16),
        in_specs=[anywhere] * 3,
        out_specs=anywhere,
        scratch_shapes=[
            pltpu.VMEM((quarter, dim), BF16),
            pltpu.VMEM((dim, dim), BF16),
            pltpu.VMEM((quarter, dim), BF16),
            pltpu.VMEM((quarter, quarter), BF16),
            pltpu.VMEM((quarter, half), BF16),
            pltpu.VMEM((half, dim), BF16),
            pltpu.VMEM((chunks, quarter, width), BF16),
            pltpu.VMEM((chunks, quarter, width), BF16),
            pltpu.VMEM((quarter, dim), BF16),
            dma((4,)),
            dma((groups,)), dma((groups,)),
            dma((4,)), dma((4,)),
            dma((groups // 2,)), dma((groups // 2,)),
            dma((chunks,)), dma((chunks,)),
            dma((groups,)), dma((groups,)),
        ],
        compiler_params=pltpu.CompilerParams(
            collective_id=0, has_side_effects=True, vmem_limit_bytes=56 * 1024 * 1024
        ),
        cost_estimate=pl.CostEstimate(
            flops=4 * quarter * dim * dim, bytes_accessed=8 * quarter * dim, transcendentals=0
        ),
    )(outgoing, a_inverse[0], b_inverse[0])
    return permute(owner, returned, False)


def solution(mesh):
    in_specs = (P(None, ("shard", "dp"), None), P(), P("dp", "shard", None), P("dp", "shard", None))
    out_specs = P(None, ("shard", "dp"), None)

    def program(gradient, owner, a_inverse, b_inverse):
        dim = gradient.shape[1]
        fits = mesh.shape["dp"] == 8 and mesh.shape["shard"] == 4 and dim % 512 == 0
        local = fused if fits and (dim // 32) % 16 == 0 else general
        return jax.shard_map(local, mesh=mesh, in_specs=in_specs, out_specs=out_specs, check_vma=False)(
            gradient, owner, a_inverse, b_inverse
        )

    return program
```

```python
import functools
import jax
import jax.numpy as jnp
from jax import lax
from jax.experimental import pallas as pl
from jax.experimental.pallas import tpu as pltpu
from jax.sharding import PartitionSpec as P

MESH = pl.DeviceIdType.MESH
F32 = jnp.float32
BF16 = jnp.bfloat16


def general(gradient, owner, a_inverse, b_inverse):
    layer_count = gradient.shape[0]
    chosen = (owner[:, None] == jnp.arange(layer_count, dtype=jnp.int32)[None, :]).astype(BF16)
    outgoing = jnp.einsum("lo,lrc->orc", chosen, gradient, preferred_element_type=F32).astype(BF16)
    owned = lax.all_to_all(outgoing, "dp", split_axis=0, concat_axis=1, tiled=True)
    right_half = jnp.dot(
        owned[0],
        lax.all_gather(b_inverse[0], "shard", axis=0, tiled=True),
        preferred_element_type=F32,
    ).astype(BF16)
    result_rows = jnp.dot(
        a_inverse[0],
        lax.all_gather(right_half, "shard", axis=0, tiled=True),
        preferred_element_type=F32,
    ).astype(BF16)
    returned = lax.all_to_all(
        result_rows[None, :, :], "dp", split_axis=1, concat_axis=0, tiled=True
    )
    return jnp.take(returned, owner, axis=0)


def move(scatter, owner_ref, in_ref, out_ref, sems):
    layers = in_ref.shape[0]
    copies = []
    for l in range(layers):
        slot = owner_ref[l]
        src, dst = (l, slot) if scatter else (slot, l)
        copies.append(pltpu.make_async_copy(in_ref.at[src], out_ref.at[dst], sems.at[l]))
        copies[-1].start()
    for copy in copies:
        copy.wait()


def permute(owner, array, scatter):
    layers, rows, dim = array.shape
    anywhere = pl.BlockSpec(memory_space=pl.ANY)
    return pl.pallas_call(
        functools.partial(move, scatter),
        out_shape=jax.ShapeDtypeStruct(array.shape, array.dtype),
        in_specs=[pl.BlockSpec(memory_space=pltpu.SMEM), anywhere],
        out_specs=anywhere,
        scratch_shapes=[pltpu.SemaphoreType.DMA((layers,))],
        cost_estimate=pl.CostEstimate(flops=0, bytes_accessed=4 * layers * rows * dim, transcendentals=0),
    )(owner, array)


def flip(index, mask):
    total, place = 0, 1
    while place <= mask:
        bit = lax.rem(index // place, 2)
        total = total + (1 - 2 * bit) * place if mask & place else total
        place *= 2
    return index + total


def dot(left, right):
    return jnp.dot(left, right, preferred_element_type=F32)


def kernel(
    groups, width, tile, side,
    g_ref, a_ref, b_ref, o_ref,
    gbuf, bfull, abuf, asib, ap, rbuf, psend, prec, obuf,
    local_sem, g_send, g_recv, b_send, b_recv, r_send, r_recv, p_send, p_recv, o_send, o_recv,
):
    _, rows, dim = g_ref.shape
    quarter, half = dim // 4, dim // 2
    d = lax.axis_index("dp")
    s = lax.axis_index("shard")
    y, c = s // 2, lax.rem(s, 2)
    sib = 2 * y + 1 - c
    across = 2 * (1 - y) + c
    across_sib = 2 * (1 - y) + 1 - c

    def rows_of(index, size, count=None):
        return pl.ds(pl.multiple_of(index * size, size), count or size)

    def remote(src, dst, send, recv, device):
        return pltpu.make_async_remote_copy(
            src_ref=src, dst_ref=dst, send_sem=send, recv_sem=recv, device_id=device, device_id_type=MESH
        )

    barrier = pltpu.get_barrier_semaphore()
    for k in range(1, groups):
        pl.semaphore_signal(barrier, inc=1, device_id=(flip(d, k), s), device_id_type=MESH)
    for other in (sib, across):
        pl.semaphore_signal(barrier, inc=1, device_id=(d, other), device_id_type=MESH)
    pl.semaphore_wait(barrier, groups + 1)

    g_copies = {}
    for k in (4, 5, 6, 7, 2, 3, 1):
        peer = flip(d, k)
        g_copies[k] = remote(
            g_ref.at[peer], gbuf.at[rows_of(d, rows)], g_send.at[k], g_recv.at[k], (peer, s)
        )
        g_copies[k].start()
    own_half = rows_of(y, half)
    other_half = rows_of(1 - y, half)
    b_across = remote(
        b_ref.at[:, own_half], bfull.at[rows_of(s, quarter), own_half], b_send.at[0], b_recv.at[0], (d, across)
    )
    b_across.start()
    b_sib = remote(b_ref, bfull.at[rows_of(s, quarter)], b_send.at[1], b_recv.at[1], (d, sib))
    b_sib.start()
    a_sib = remote(a_ref.at[:, rows_of(across_sib, quarter)], asib, b_send.at[2], b_recv.at[2], (d, sib))
    a_sib.start()
    a_own = pltpu.make_async_copy(a_ref, abuf, local_sem.at[0])
    a_own.start()
    b_own = pltpu.make_async_copy(b_ref, bfull.at[rows_of(s, quarter)], local_sem.at[1])
    b_own.start()
    g_own = pltpu.make_async_copy(g_ref.at[d], gbuf.at[rows_of(d, rows)], local_sem.at[2])
    g_own.start()

    a_own.wait()
    per = quarter // side

    def turn_own(i, carry):
        u, v = i // per, lax.rem(i, per)
        block = abuf[rows_of(u, side), pl.ds(pl.multiple_of(across * quarter + v * side, side), side)]
        ap[rows_of(v, side), pl.ds(pl.multiple_of(c * quarter + u * side, side), side)] = block.T
        return carry

    lax.fori_loop(0, per * per, turn_own, 0)
    a_sib.wait_recv()

    def turn_sib(i, carry):
        u, v = i // per, lax.rem(i, per)
        block = asib[rows_of(u, side), rows_of(v, side)]
        ap[rows_of(v, side), pl.ds(pl.multiple_of((1 - c) * quarter + u * side, side), side)] = block.T
        return carry

    lax.fori_loop(0, per * per, turn_sib, 0)

    b_own.wait()
    b_sib.wait_recv()
    wide = half // side

    def turn_b(i, carry):
        u, v = i // wide, lax.rem(i, wide)
        block = bfull[
            pl.ds(pl.multiple_of(y * half + u * side, side), side),
            pl.ds(pl.multiple_of((1 - y) * half + v * side, side), side),
        ]
        bfull[
            pl.ds(pl.multiple_of((1 - y) * half + v * side, side), side),
            pl.ds(pl.multiple_of(y * half + u * side, side), side),
        ] = block.T
        return carry

    lax.fori_loop(0, wide * wide, turn_b, 0)

    arrived = bfull.at[rows_of(across, quarter), other_half]
    remote(arrived, arrived, b_send.at[0], b_recv.at[0], (d, across)).wait_recv()
    relay = remote(arrived, arrived, b_send.at[3], b_recv.at[3], (d, sib))
    relay.start()
    relay.wait_recv()

    pair = 2 * rows
    r_copies = []
    for step in range(groups // 2):
        first = flip(d // 2, step)
        if step == 0:
            g_own.wait()
            g_copies[1].wait_recv()
        else:
            g_copies[2 * step].wait_recv()
            g_copies[2 * step + 1].wait_recv()
        here = pl.ds(pl.multiple_of(c * quarter + first * pair, pair), pair)

        def product(t, carry, first=first, here=here):
            columns = rows_of(t, tile)
            rbuf[here, columns] = dot(gbuf[rows_of(first, pair), :], bfull[:, columns]).astype(BF16)
            return carry

        lax.fori_loop(0, dim // tile, product, 0)
        copy = remote(rbuf.at[here], rbuf.at[here], r_send.at[step], r_recv.at[step], (d, sib))
        copy.start()
        r_copies.append(copy)
    for copy in r_copies:
        copy.wait_recv()

    chunks = dim // width
    pieces = 2 * chunks
    z_half = d // (groups // 2)
    piece_rows = quarter // 2

    def place(i):
        late = i // chunks
        target = late * z_half + (1 - late) * (1 - z_half)
        return late, target, rows_of(target, piece_rows), rows_of(i - late * chunks, width)

    def partial(i):
        return remote(psend.at[i], prec.at[i], p_send.at[i], p_recv.at[i], (d, across))

    def give(i):
        _, _, here, columns = place(i)
        psend[i] = dot(ap[here, :], rbuf[:, columns]).astype(BF16)
        partial(i).start()

    def finish(i, carry):
        late, target, here, columns = place(i)
        mine = dot(abuf[here, own_half], rbuf[:, columns])
        partial(i).wait_recv()
        obuf[here, columns] = (mine + prec[i].astype(F32)).astype(BF16)
        for q in range(groups // 2):
            peer = target * (groups // 2) + lax.rem(flip(d, q), groups // 2)
            k = (1 - late) * (groups // 2) + q

            def send(peer=peer, k=k):
                remote(
                    obuf.at[rows_of(peer, rows), columns], o_ref.at[d, :, columns],
                    o_send.at[k], o_recv.at[k], (peer, s),
                ).start()

            if q == 0:
                pl.when(late == 0)(send)
            else:
                send()

        @pl.when(i + lead < pieces)
        def _():
            give(i + lead)

        return carry

    lead = 4
    for i in range(lead):
        give(i)
    lax.fori_loop(0, pieces, finish, 0)
    o_own = pltpu.make_async_copy(obuf.at[rows_of(d, rows)], o_ref.at[d], local_sem.at[3])
    o_own.start()

    for k in range(1, groups):
        g_copies[k].wait_send()
    for copy in (b_across, b_sib, a_sib, relay, *r_copies):
        copy.wait_send()

    def sent(i, carry):
        partial(i).wait_send()
        return carry

    lax.fori_loop(0, pieces, sent, 0)
    o_own.wait()
    for k in range(1, groups):
        peer = flip(d, k)
        whole = remote(obuf.at[rows_of(peer, rows)], o_ref.at[peer], o_send.at[k], o_recv.at[k], (peer, s))
        whole.wait_send()
        whole.wait_recv()


def fused(gradient, owner, a_inverse, b_inverse):
    groups, rows, dim = gradient.shape
    quarter, half = dim // 4, dim // 2
    width, tile, side = 256, 512, 128
    chunks = dim // width
    outgoing = permute(owner, gradient, True)
    anywhere = pl.BlockSpec(memory_space=pl.ANY)
    dma = pltpu.SemaphoreType.DMA
    returned = pl.pallas_call(
        functools.partial(kernel, groups, width, tile, side),
        out_shape=jax.ShapeDtypeStruct(gradient.shape, BF16),
        in_specs=[anywhere] * 3,
        out_specs=anywhere,
        scratch_shapes=[
            pltpu.VMEM((quarter, dim), BF16),
            pltpu.VMEM((dim, dim), BF16),
            pltpu.VMEM((quarter, dim), BF16),
            pltpu.VMEM((quarter, quarter), BF16),
            pltpu.VMEM((quarter, half), BF16),
            pltpu.VMEM((half, dim), BF16),
            pltpu.VMEM((2 * chunks, quarter // 2, width), BF16),
            pltpu.VMEM((2 * chunks, quarter // 2, width), BF16),
            pltpu.VMEM((quarter, dim), BF16),
            dma((4,)),
            dma((groups,)), dma((groups,)),
            dma((4,)), dma((4,)),
            dma((groups // 2,)), dma((groups // 2,)),
            dma((2 * chunks,)), dma((2 * chunks,)),
            dma((groups,)), dma((groups,)),
        ],
        compiler_params=pltpu.CompilerParams(
            collective_id=0, has_side_effects=True, vmem_limit_bytes=56 * 1024 * 1024
        ),
        cost_estimate=pl.CostEstimate(
            flops=4 * quarter * dim * dim, bytes_accessed=8 * quarter * dim, transcendentals=0
        ),
    )(outgoing, a_inverse[0], b_inverse[0])
    return permute(owner, returned, False)


def solution(mesh):
    in_specs = (P(None, ("shard", "dp"), None), P(), P("dp", "shard", None), P("dp", "shard", None))
    out_specs = P(None, ("shard", "dp"), None)

    def program(gradient, owner, a_inverse, b_inverse):
        dim = gradient.shape[1]
        fits = mesh.shape["dp"] == 8 and mesh.shape["shard"] == 4 and dim % 512 == 0
        local = fused if fits and (dim // 32) % 16 == 0 else general
        return jax.shard_map(local, mesh=mesh, in_specs=in_specs, out_specs=out_specs, check_vma=False)(
            gradient, owner, a_inverse, b_inverse
        )

    return program
```

```python
import functools
import jax
import jax.numpy as jnp
from jax import lax
from jax.experimental import pallas as pl
from jax.experimental.pallas import tpu as pltpu
from jax.sharding import PartitionSpec as P

MESH = pl.DeviceIdType.MESH
F32 = jnp.float32
BF16 = jnp.bfloat16


def general(gradient, owner, a_inverse, b_inverse):
    layer_count = gradient.shape[0]
    chosen = (owner[:, None] == jnp.arange(layer_count, dtype=jnp.int32)[None, :]).astype(BF16)
    outgoing = jnp.einsum("lo,lrc->orc", chosen, gradient, preferred_element_type=F32).astype(BF16)
    owned = lax.all_to_all(outgoing, "dp", split_axis=0, concat_axis=1, tiled=True)
    right_half = jnp.dot(
        owned[0],
        lax.all_gather(b_inverse[0], "shard", axis=0, tiled=True),
        preferred_element_type=F32,
    ).astype(BF16)
    result_rows = jnp.dot(
        a_inverse[0],
        lax.all_gather(right_half, "shard", axis=0, tiled=True),
        preferred_element_type=F32,
    ).astype(BF16)
    returned = lax.all_to_all(
        result_rows[None, :, :], "dp", split_axis=1, concat_axis=0, tiled=True
    )
    return jnp.take(returned, owner, axis=0)


def collect(owner_ref, in_ref, out_ref, held, in_sems, out_sems):
    layers = in_ref.shape[0]
    loads = []
    for l in range(layers):
        loads.append(pltpu.make_async_copy(in_ref.at[owner_ref[l]], held.at[l], in_sems.at[l]))
        loads[-1].start()
    stores = []
    for l in range(layers):
        loads[l].wait()
        stores.append(pltpu.make_async_copy(held.at[l], out_ref.at[l], out_sems.at[l]))
        stores[-1].start()
    for store in stores:
        store.wait()


def to_layers(owner, array):
    layers, rows, dim = array.shape
    anywhere = pl.BlockSpec(memory_space=pl.ANY)
    return pl.pallas_call(
        collect,
        out_shape=jax.ShapeDtypeStruct(array.shape, array.dtype),
        in_specs=[pl.BlockSpec(memory_space=pltpu.SMEM), anywhere],
        out_specs=anywhere,
        scratch_shapes=[
            pltpu.VMEM(array.shape, array.dtype),
            pltpu.SemaphoreType.DMA((layers,)),
            pltpu.SemaphoreType.DMA((layers,)),
        ],
        cost_estimate=pl.CostEstimate(flops=0, bytes_accessed=4 * layers * rows * dim, transcendentals=0),
    )(owner, array)


def flip(index, mask):
    total, place = 0, 1
    while place <= mask:
        bit = lax.rem(index // place, 2)
        total = total + (1 - 2 * bit) * place if mask & place else total
        place *= 2
    return index + total


def dot(left, right):
    return jnp.dot(left, right, preferred_element_type=F32)


def kernel(
    groups, width, tile, side,
    owner_ref, g_ref, a_ref, b_ref, o_ref,
    gsend, gbuf, acc, bfull, abuf, asib, ap, rbuf, psend, prec, obuf,
    local_sem, g_send, g_recv, b_send, b_recv, r_send, r_recv, p_send, p_recv, o_send, o_recv,
):
    _, rows, dim = g_ref.shape
    quarter, half = dim // 4, dim // 2
    d = lax.axis_index("dp")
    s = lax.axis_index("shard")
    y, c = s // 2, lax.rem(s, 2)
    sib = 2 * y + 1 - c
    across = 2 * (1 - y) + c
    across_sib = 2 * (1 - y) + 1 - c

    def rows_of(index, size, count=None):
        return pl.ds(pl.multiple_of(index * size, size), count or size)

    def remote(src, dst, send, recv, device):
        return pltpu.make_async_remote_copy(
            src_ref=src, dst_ref=dst, send_sem=send, recv_sem=recv, device_id=device, device_id_type=MESH
        )

    barrier = pltpu.get_barrier_semaphore()
    for k in range(1, groups):
        pl.semaphore_signal(barrier, inc=1, device_id=(flip(d, k), s), device_id_type=MESH)
    for other in (sib, across):
        pl.semaphore_signal(barrier, inc=1, device_id=(d, other), device_id_type=MESH)
    pl.semaphore_wait(barrier, groups + 1)

    own_half = rows_of(y, half)
    other_half = rows_of(1 - y, half)
    b_across = remote(
        b_ref.at[:, own_half], bfull.at[rows_of(s, quarter), own_half], b_send.at[0], b_recv.at[0], (d, across)
    )
    b_across.start()
    b_sib = remote(b_ref, bfull.at[rows_of(s, quarter)], b_send.at[1], b_recv.at[1], (d, sib))
    b_sib.start()
    a_sib = remote(a_ref.at[:, rows_of(across_sib, quarter)], asib, b_send.at[2], b_recv.at[2], (d, sib))
    a_sib.start()
    a_own = pltpu.make_async_copy(a_ref, abuf, local_sem.at[0])
    a_own.start()
    b_own = pltpu.make_async_copy(b_ref, bfull.at[rows_of(s, quarter)], local_sem.at[1])
    b_own.start()

    def layer_of(slot):
        found = 0
        for l in range(groups):
            found = jnp.where(owner_ref[l] == slot, l, found)
        return found

    parts = (s, sib, across, across_sib)
    order = (4, 2, 5, 3, 6, 1, 7)

    def gradient_copy(part, k):
        peer, columns = flip(d, k), rows_of(parts[part], quarter)
        return remote(
            gsend.at[k, :, columns], gbuf.at[rows_of(d, rows), columns],
            g_send.at[part, k], g_recv.at[part, k], (peer, s),
        )

    def arrival(part, k):
        peer, columns = flip(d, k), rows_of(parts[part], quarter)
        return remote(
            gsend.at[k, :, columns], gbuf.at[rows_of(peer, rows), columns],
            g_send.at[part, k], g_recv.at[part, k], (peer, s),
        )

    for k in order:
        gsend[k] = g_ref[layer_of(flip(d, k))]
        gradient_copy(0, k).start()
    for part in range(1, 4):
        for k in order:
            gradient_copy(part, k).start()
    gbuf[rows_of(d, rows), :] = g_ref[layer_of(d)]

    a_own.wait()
    per = quarter // side

    def turn_own(i, carry):
        u, v = i // per, lax.rem(i, per)
        block = abuf[rows_of(u, side), pl.ds(pl.multiple_of(across * quarter + v * side, side), side)]
        ap[rows_of(v, side), pl.ds(pl.multiple_of(c * quarter + u * side, side), side)] = block.T
        return carry

    lax.fori_loop(0, per * per, turn_own, 0)
    a_sib.wait_recv()

    def turn_sib(i, carry):
        u, v = i // per, lax.rem(i, per)
        block = asib[rows_of(u, side), rows_of(v, side)]
        ap[rows_of(v, side), pl.ds(pl.multiple_of((1 - c) * quarter + u * side, side), side)] = block.T
        return carry

    lax.fori_loop(0, per * per, turn_sib, 0)

    b_own.wait()
    b_sib.wait_recv()
    wide = half // side

    def turn_b(i, carry):
        u, v = i // wide, lax.rem(i, wide)
        block = bfull[
            pl.ds(pl.multiple_of(y * half + u * side, side), side),
            pl.ds(pl.multiple_of((1 - y) * half + v * side, side), side),
        ]
        bfull[
            pl.ds(pl.multiple_of((1 - y) * half + v * side, side), side),
            pl.ds(pl.multiple_of(y * half + u * side, side), side),
        ] = block.T
        return carry

    lax.fori_loop(0, wide * wide, turn_b, 0)

    def add_part(part):
        for k in order:
            arrival(part, k).wait_recv()
        depth = rows_of(parts[part], quarter)

        def product(t, carry):
            columns = rows_of(t, tile)
            term = dot(gbuf[:, depth], bfull[depth, columns])
            if part == 0:
                acc[:, columns] = term
            elif part < 3:
                acc[:, columns] += term
            else:
                rbuf[here, columns] = (acc[:, columns] + term).astype(BF16)
                half_copy(t).start()
            return carry

        lax.fori_loop(0, dim // tile, product, 0)

    here = rows_of(c, quarter)

    def half_copy(t):
        block = rbuf.at[here, rows_of(t, tile)]
        return remote(block, block, r_send.at[t], r_recv.at[t], (d, sib))

    add_part(0)
    add_part(1)

    arrived = bfull.at[rows_of(across, quarter), other_half]
    remote(arrived, arrived, b_send.at[0], b_recv.at[0], (d, across)).wait_recv()
    relay = remote(arrived, arrived, b_send.at[3], b_recv.at[3], (d, sib))
    relay.start()
    add_part(2)
    relay.wait_recv()
    add_part(3)

    chunks = dim // width
    pieces = 2 * chunks
    z_half = d // (groups // 2)
    piece_rows = quarter // 2

    def place(i):
        late = lax.rem(i, 2)
        target = late * z_half + (1 - late) * (1 - z_half)
        return late, target, rows_of(target, piece_rows), rows_of(i // 2, width)

    def partial(i):
        return remote(psend.at[i], prec.at[i], p_send.at[i], p_recv.at[i], (d, across))

    per_tile = 2 * tile // width

    def give(i):
        _, _, here, columns = place(i)

        @pl.when(lax.rem(i, per_tile) == 0)
        def _():
            half_copy(i // per_tile).wait_recv()

        psend[i] = dot(ap[here, :], rbuf[:, columns]).astype(BF16)
        partial(i).start()

    def finish(i, carry):
        late, target, here, columns = place(i)
        mine = dot(abuf[here, own_half], rbuf[:, columns])
        partial(i).wait_recv()
        obuf[here, columns] = (mine + prec[i].astype(F32)).astype(BF16)
        for q in range(groups // 2):
            peer = target * (groups // 2) + lax.rem(flip(d, q), groups // 2)
            k = (1 - late) * (groups // 2) + q

            def send(peer=peer, k=k):
                remote(
                    obuf.at[rows_of(peer, rows), columns], o_ref.at[d, :, columns],
                    o_send.at[k], o_recv.at[k], (peer, s),
                ).start()

            if q == 0:
                pl.when(late == 0)(send)
            else:
                send()

        @pl.when(i + lead < pieces)
        def _():
            give(i + lead)

        return carry

    lead = 4
    for i in range(lead):
        give(i)
    lax.fori_loop(0, pieces, finish, 0)
    o_own = pltpu.make_async_copy(obuf.at[rows_of(d, rows)], o_ref.at[d], local_sem.at[3])
    o_own.start()

    for part in range(4):
        for k in order:
            gradient_copy(part, k).wait_send()
    for t in range(dim // tile):
        half_copy(t).wait_send()
    for copy in (b_across, b_sib, a_sib, relay):
        copy.wait_send()

    def sent(i, carry):
        partial(i).wait_send()
        return carry

    lax.fori_loop(0, pieces, sent, 0)
    o_own.wait()
    for k in range(1, groups):
        peer = flip(d, k)
        whole = remote(obuf.at[rows_of(peer, rows)], o_ref.at[peer], o_send.at[k], o_recv.at[k], (peer, s))
        whole.wait_send()
        whole.wait_recv()


def fused(gradient, owner, a_inverse, b_inverse):
    groups, rows, dim = gradient.shape
    quarter, half = dim // 4, dim // 2
    width, tile, side = 256, 512, 128
    chunks = dim // width
    anywhere = pl.BlockSpec(memory_space=pl.ANY)
    dma = pltpu.SemaphoreType.DMA
    returned = pl.pallas_call(
        functools.partial(kernel, groups, width, tile, side),
        out_shape=jax.ShapeDtypeStruct(gradient.shape, BF16),
        in_specs=[pl.BlockSpec(memory_space=pltpu.SMEM), pl.BlockSpec(memory_space=pltpu.VMEM), anywhere, anywhere],
        out_specs=anywhere,
        scratch_shapes=[
            pltpu.VMEM(gradient.shape, BF16),
            pltpu.VMEM((quarter, dim), BF16),
            pltpu.VMEM((quarter, dim), F32),
            pltpu.VMEM((dim, dim), BF16),
            pltpu.VMEM((quarter, dim), BF16),
            pltpu.VMEM((quarter, quarter), BF16),
            pltpu.VMEM((quarter, half), BF16),
            pltpu.VMEM((half, dim), BF16),
            pltpu.VMEM((2 * chunks, quarter // 2, width), BF16),
            pltpu.VMEM((2 * chunks, quarter // 2, width), BF16),
            pltpu.VMEM((quarter, dim), BF16),
            dma((4,)),
            dma((4, groups)), dma((4, groups)),
            dma((4,)), dma((4,)),
            dma((dim // tile,)), dma((dim // tile,)),
            dma((2 * chunks,)), dma((2 * chunks,)),
            dma((groups,)), dma((groups,)),
        ],
        compiler_params=pltpu.CompilerParams(
            collective_id=0, has_side_effects=True, vmem_limit_bytes=60 * 1024 * 1024
        ),
        cost_estimate=pl.CostEstimate(
            flops=4 * quarter * dim * dim, bytes_accessed=8 * quarter * dim, transcendentals=0
        ),
    )(owner, gradient, a_inverse[0], b_inverse[0])
    return to_layers(owner, returned)


def solution(mesh):
    in_specs = (P(None, ("shard", "dp"), None), P(), P("dp", "shard", None), P("dp", "shard", None))
    out_specs = P(None, ("shard", "dp"), None)

    def program(gradient, owner, a_inverse, b_inverse):
        dim = gradient.shape[1]
        fits = mesh.shape["dp"] == 8 and mesh.shape["shard"] == 4 and dim % 512 == 0
        local = fused if fits and (dim // 32) % 16 == 0 else general
        return jax.shard_map(local, mesh=mesh, in_specs=in_specs, out_specs=out_specs, check_vma=False)(
            gradient, owner, a_inverse, b_inverse
        )

    return program
```

```python
import functools
import jax
import jax.numpy as jnp
from jax import lax
from jax.experimental import pallas as pl
from jax.experimental.pallas import tpu as pltpu
from jax.sharding import PartitionSpec as P

MESH = pl.DeviceIdType.MESH
F32 = jnp.float32
BF16 = jnp.bfloat16


def general(gradient, owner, a_inverse, b_inverse):
    layer_count = gradient.shape[0]
    chosen = (owner[:, None] == jnp.arange(layer_count, dtype=jnp.int32)[None, :]).astype(BF16)
    outgoing = jnp.einsum("lo,lrc->orc", chosen, gradient, preferred_element_type=F32).astype(BF16)
    owned = lax.all_to_all(outgoing, "dp", split_axis=0, concat_axis=1, tiled=True)
    right_half = jnp.dot(
        owned[0],
        lax.all_gather(b_inverse[0], "shard", axis=0, tiled=True),
        preferred_element_type=F32,
    ).astype(BF16)
    result_rows = jnp.dot(
        a_inverse[0],
        lax.all_gather(right_half, "shard", axis=0, tiled=True),
        preferred_element_type=F32,
    ).astype(BF16)
    returned = lax.all_to_all(
        result_rows[None, :, :], "dp", split_axis=1, concat_axis=0, tiled=True
    )
    return jnp.take(returned, owner, axis=0)


def collect(owner_ref, in_ref, out_ref, held, in_sems, out_sems):
    layers = in_ref.shape[0]
    loads = []
    for l in range(layers):
        loads.append(pltpu.make_async_copy(in_ref.at[owner_ref[l]], held.at[l], in_sems.at[l]))
        loads[-1].start()
    stores = []
    for l in range(layers):
        loads[l].wait()
        stores.append(pltpu.make_async_copy(held.at[l], out_ref.at[l], out_sems.at[l]))
        stores[-1].start()
    for store in stores:
        store.wait()


def to_layers(owner, array):
    layers, rows, dim = array.shape
    anywhere = pl.BlockSpec(memory_space=pl.ANY)
    return pl.pallas_call(
        collect,
        out_shape=jax.ShapeDtypeStruct(array.shape, array.dtype),
        in_specs=[pl.BlockSpec(memory_space=pltpu.SMEM), anywhere],
        out_specs=anywhere,
        scratch_shapes=[
            pltpu.VMEM(array.shape, array.dtype),
            pltpu.SemaphoreType.DMA((layers,)),
            pltpu.SemaphoreType.DMA((layers,)),
        ],
        cost_estimate=pl.CostEstimate(flops=0, bytes_accessed=4 * layers * rows * dim, transcendentals=0),
    )(owner, array)


def flip(index, mask):
    total, place = 0, 1
    while place <= mask:
        bit = lax.rem(index // place, 2)
        total = total + (1 - 2 * bit) * place if mask & place else total
        place *= 2
    return index + total


def dot(left, right):
    return jnp.dot(left, right, preferred_element_type=F32)


def kernel(
    groups, width, tile, side,
    owner_ref, g_ref, a_ref, b_ref, o_ref,
    gin, gsend, gbuf, acc, bfull, abuf, asib, ap, rbuf, psend, prec, obuf,
    local_sem, g_send, g_recv, b_send, b_recv, r_send, r_recv, p_send, p_recv, o_send, o_recv,
):
    _, rows, dim = g_ref.shape
    quarter, half = dim // 4, dim // 2
    d = lax.axis_index("dp")
    s = lax.axis_index("shard")
    y, c = s // 2, lax.rem(s, 2)
    sib = 2 * y + 1 - c
    across = 2 * (1 - y) + c
    across_sib = 2 * (1 - y) + 1 - c

    def rows_of(index, size, count=None):
        return pl.ds(pl.multiple_of(index * size, size), count or size)

    def remote(src, dst, send, recv, device):
        return pltpu.make_async_remote_copy(
            src_ref=src, dst_ref=dst, send_sem=send, recv_sem=recv, device_id=device, device_id_type=MESH
        )

    g_in = pltpu.make_async_copy(g_ref, gin, local_sem.at[2])
    g_in.start()
    a_own = pltpu.make_async_copy(a_ref, abuf, local_sem.at[0])
    a_own.start()
    b_own = pltpu.make_async_copy(b_ref, bfull.at[rows_of(s, quarter)], local_sem.at[1])
    b_own.start()

    barrier = pltpu.get_barrier_semaphore()
    for k in range(1, groups):
        pl.semaphore_signal(barrier, inc=1, device_id=(flip(d, k), s), device_id_type=MESH)
    for other in (sib, across):
        pl.semaphore_signal(barrier, inc=1, device_id=(d, other), device_id_type=MESH)
    pl.semaphore_wait(barrier, groups + 1)

    own_half = rows_of(y, half)
    other_half = rows_of(1 - y, half)
    def layer_of(slot):
        found = 0
        for l in range(groups):
            found = jnp.where(owner_ref[l] == slot, l, found)
        return found

    parts = (s, sib, across, across_sib)
    order = (4, 2, 5, 3, 6, 1, 7)

    def gradient_copy(part, k):
        peer, columns = flip(d, k), rows_of(parts[part], quarter)
        return remote(
            gsend.at[k, :, columns], gbuf.at[rows_of(d, rows), columns],
            g_send.at[part, k], g_recv.at[part, k], (peer, s),
        )

    def arrival(part, k):
        peer, columns = flip(d, k), rows_of(parts[part], quarter)
        return remote(
            gsend.at[k, :, columns], gbuf.at[rows_of(peer, rows), columns],
            g_send.at[part, k], g_recv.at[part, k], (peer, s),
        )

    g_in.wait()
    for k in order:
        gsend[k] = gin[layer_of(flip(d, k))]
        gradient_copy(0, k).start()
    b_across = remote(
        b_ref.at[:, own_half], bfull.at[rows_of(s, quarter), own_half], b_send.at[0], b_recv.at[0], (d, across)
    )
    b_across.start()
    b_sib = remote(b_ref, bfull.at[rows_of(s, quarter)], b_send.at[1], b_recv.at[1], (d, sib))
    b_sib.start()
    a_sib = remote(a_ref.at[:, rows_of(across_sib, quarter)], asib, b_send.at[2], b_recv.at[2], (d, sib))
    a_sib.start()
    for part in range(1, 4):
        for k in order:
            gradient_copy(part, k).start()
    gbuf[rows_of(d, rows), :] = gin[layer_of(d)]

    a_own.wait()
    per = quarter // side

    def turn_own(i, carry):
        u, v = i // per, lax.rem(i, per)
        block = abuf[rows_of(u, side), pl.ds(pl.multiple_of(across * quarter + v * side, side), side)]
        ap[rows_of(v, side), pl.ds(pl.multiple_of(c * quarter + u * side, side), side)] = block.T
        return carry

    lax.fori_loop(0, per * per, turn_own, 0)
    a_sib.wait_recv()

    def turn_sib(i, carry):
        u, v = i // per, lax.rem(i, per)
        block = asib[rows_of(u, side), rows_of(v, side)]
        ap[rows_of(v, side), pl.ds(pl.multiple_of((1 - c) * quarter + u * side, side), side)] = block.T
        return carry

    lax.fori_loop(0, per * per, turn_sib, 0)

    b_own.wait()
    b_sib.wait_recv()
    wide = half // side

    def turn_b(i, carry):
        u, v = i // wide, lax.rem(i, wide)
        block = bfull[
            pl.ds(pl.multiple_of(y * half + u * side, side), side),
            pl.ds(pl.multiple_of((1 - y) * half + v * side, side), side),
        ]
        bfull[
            pl.ds(pl.multiple_of((1 - y) * half + v * side, side), side),
            pl.ds(pl.multiple_of(y * half + u * side, side), side),
        ] = block.T
        return carry

    lax.fori_loop(0, wide * wide, turn_b, 0)

    def add_part(part):
        for k in order:
            arrival(part, k).wait_recv()
        depth = rows_of(parts[part], quarter)

        def product(t, carry):
            columns = rows_of(t, tile)
            term = dot(gbuf[:, depth], bfull[depth, columns])
            if part == 0:
                acc[:, columns] = term
            elif part < 3:
                acc[:, columns] += term
            else:
                rbuf[here, columns] = (acc[:, columns] + term).astype(BF16)
                half_copy(t).start()
            return carry

        lax.fori_loop(0, dim // tile, product, 0)

    here = rows_of(c, quarter)

    def half_copy(t):
        block = rbuf.at[here, rows_of(t, tile)]
        return remote(block, block, r_send.at[t], r_recv.at[t], (d, sib))

    add_part(0)
    add_part(1)

    arrived = bfull.at[rows_of(across, quarter), other_half]
    remote(arrived, arrived, b_send.at[0], b_recv.at[0], (d, across)).wait_recv()
    relay = remote(arrived, arrived, b_send.at[3], b_recv.at[3], (d, sib))
    relay.start()
    add_part(2)
    relay.wait_recv()
    add_part(3)

    chunks = dim // width
    pieces = 2 * chunks
    z_half = d // (groups // 2)
    piece_rows = quarter // 2

    def place(i):
        late = lax.rem(i, 2)
        target = late * z_half + (1 - late) * (1 - z_half)
        return late, target, rows_of(target, piece_rows), rows_of(i // 2, width)

    def partial(i):
        return remote(psend.at[i], prec.at[i], p_send.at[i], p_recv.at[i], (d, across))

    per_tile = 2 * tile // width

    def give(i):
        _, _, here, columns = place(i)

        @pl.when(lax.rem(i, per_tile) == 0)
        def _():
            half_copy(i // per_tile).wait_recv()

        psend[i] = dot(ap[here, :], rbuf[:, columns]).astype(BF16)
        partial(i).start()

    def finish(i, carry):
        late, target, here, columns = place(i)
        mine = dot(abuf[here, own_half], rbuf[:, columns])
        partial(i).wait_recv()
        obuf[here, columns] = (mine + prec[i].astype(F32)).astype(BF16)
        for q in range(groups // 2):
            peer = target * (groups // 2) + lax.rem(flip(d, q), groups // 2)
            k = (1 - late) * (groups // 2) + q

            def send(peer=peer, k=k):
                remote(
                    obuf.at[rows_of(peer, rows), columns], o_ref.at[d, :, columns],
                    o_send.at[k], o_recv.at[k], (peer, s),
                ).start()

            if q == 0:
                pl.when(late == 0)(send)
            else:
                send()

        @pl.when(i + lead < pieces)
        def _():
            give(i + lead)

        return carry

    lead = 4
    for i in range(lead):
        give(i)
    lax.fori_loop(0, pieces, finish, 0)
    o_own = pltpu.make_async_copy(obuf.at[rows_of(d, rows)], o_ref.at[d], local_sem.at[3])
    o_own.start()

    for part in range(4):
        for k in order:
            gradient_copy(part, k).wait_send()
    for t in range(dim // tile):
        half_copy(t).wait_send()
    for copy in (b_across, b_sib, a_sib, relay):
        copy.wait_send()

    def sent(i, carry):
        partial(i).wait_send()
        return carry

    lax.fori_loop(0, pieces, sent, 0)
    o_own.wait()
    for k in range(1, groups):
        peer = flip(d, k)
        whole = remote(obuf.at[rows_of(peer, rows)], o_ref.at[peer], o_send.at[k], o_recv.at[k], (peer, s))
        whole.wait_send()
        whole.wait_recv()


def fused(gradient, owner, a_inverse, b_inverse):
    groups, rows, dim = gradient.shape
    quarter, half = dim // 4, dim // 2
    width, tile, side = 256, 256, 128
    chunks = dim // width
    anywhere = pl.BlockSpec(memory_space=pl.ANY)
    dma = pltpu.SemaphoreType.DMA
    returned = pl.pallas_call(
        functools.partial(kernel, groups, width, tile, side),
        out_shape=jax.ShapeDtypeStruct(gradient.shape, BF16),
        in_specs=[pl.BlockSpec(memory_space=pltpu.SMEM), anywhere, anywhere, anywhere],
        out_specs=anywhere,
        scratch_shapes=[
            pltpu.VMEM(gradient.shape, BF16),
            pltpu.VMEM(gradient.shape, BF16),
            pltpu.VMEM((quarter, dim), BF16),
            pltpu.VMEM((quarter, dim), F32),
            pltpu.VMEM((dim, dim), BF16),
            pltpu.VMEM((quarter, dim), BF16),
            pltpu.VMEM((quarter, quarter), BF16),
            pltpu.VMEM((quarter, half), BF16),
            pltpu.VMEM((half, dim), BF16),
            pltpu.VMEM((2 * chunks, quarter // 2, width), BF16),
            pltpu.VMEM((2 * chunks, quarter // 2, width), BF16),
            pltpu.VMEM((quarter, dim), BF16),
            dma((4,)),
            dma((4, groups)), dma((4, groups)),
            dma((4,)), dma((4,)),
            dma((dim // tile,)), dma((dim // tile,)),
            dma((2 * chunks,)), dma((2 * chunks,)),
            dma((groups,)), dma((groups,)),
        ],
        compiler_params=pltpu.CompilerParams(
            collective_id=0, has_side_effects=True, vmem_limit_bytes=60 * 1024 * 1024
        ),
        cost_estimate=pl.CostEstimate(
            flops=4 * quarter * dim * dim, bytes_accessed=8 * quarter * dim, transcendentals=0
        ),
    )(owner, gradient, a_inverse[0], b_inverse[0])
    return to_layers(owner, returned)


def solution(mesh):
    in_specs = (P(None, ("shard", "dp"), None), P(), P("dp", "shard", None), P("dp", "shard", None))
    out_specs = P(None, ("shard", "dp"), None)

    def program(gradient, owner, a_inverse, b_inverse):
        dim = gradient.shape[1]
        fits = mesh.shape["dp"] == 8 and mesh.shape["shard"] == 4 and dim % 512 == 0
        local = fused if fits and (dim // 32) % 16 == 0 else general
        return jax.shard_map(local, mesh=mesh, in_specs=in_specs, out_specs=out_specs, check_vma=False)(
            gradient, owner, a_inverse, b_inverse
        )

    return program
```

```python
import functools
import jax
import jax.numpy as jnp
from jax import lax
from jax.experimental import pallas as pl
from jax.experimental.pallas import tpu as pltpu
from jax.sharding import PartitionSpec as P

MESH = pl.DeviceIdType.MESH
F32 = jnp.float32
BF16 = jnp.bfloat16


def general(gradient, owner, a_inverse, b_inverse):
    layer_count = gradient.shape[0]
    chosen = (owner[:, None] == jnp.arange(layer_count, dtype=jnp.int32)[None, :]).astype(BF16)
    outgoing = jnp.einsum("lo,lrc->orc", chosen, gradient, preferred_element_type=F32).astype(BF16)
    owned = lax.all_to_all(outgoing, "dp", split_axis=0, concat_axis=1, tiled=True)
    right_half = jnp.dot(
        owned[0],
        lax.all_gather(b_inverse[0], "shard", axis=0, tiled=True),
        preferred_element_type=F32,
    ).astype(BF16)
    result_rows = jnp.dot(
        a_inverse[0],
        lax.all_gather(right_half, "shard", axis=0, tiled=True),
        preferred_element_type=F32,
    ).astype(BF16)
    returned = lax.all_to_all(
        result_rows[None, :, :], "dp", split_axis=1, concat_axis=0, tiled=True
    )
    return jnp.take(returned, owner, axis=0)


def collect(owner_ref, in_ref, out_ref, held, in_sems, out_sems):
    layers = in_ref.shape[0]
    loads = []
    for l in range(layers):
        loads.append(pltpu.make_async_copy(in_ref.at[owner_ref[l]], held.at[l], in_sems.at[l]))
        loads[-1].start()
    stores = []
    for l in range(layers):
        loads[l].wait()
        stores.append(pltpu.make_async_copy(held.at[l], out_ref.at[l], out_sems.at[l]))
        stores[-1].start()
    for store in stores:
        store.wait()


def to_layers(owner, array):
    layers, rows, dim = array.shape
    anywhere = pl.BlockSpec(memory_space=pl.ANY)
    return pl.pallas_call(
        collect,
        out_shape=jax.ShapeDtypeStruct(array.shape, array.dtype),
        in_specs=[pl.BlockSpec(memory_space=pltpu.SMEM), anywhere],
        out_specs=anywhere,
        scratch_shapes=[
            pltpu.VMEM(array.shape, array.dtype),
            pltpu.SemaphoreType.DMA((layers,)),
            pltpu.SemaphoreType.DMA((layers,)),
        ],
        cost_estimate=pl.CostEstimate(flops=0, bytes_accessed=4 * layers * rows * dim, transcendentals=0),
    )(owner, array)


def flip(index, mask):
    total, place = 0, 1
    while place <= mask:
        bit = lax.rem(index // place, 2)
        total = total + (1 - 2 * bit) * place if mask & place else total
        place *= 2
    return index + total


def dot(left, right):
    return jnp.dot(left, right, preferred_element_type=F32)


def kernel(
    groups, width, tile, side,
    owner_ref, g_ref, a_ref, b_ref, o_ref,
    gin, gsend, gbuf, acc, bfull, abuf, asib, ap, rbuf, psend, prec, obuf,
    local_sem, g_send, g_recv, b_send, b_recv, r_send, r_recv, p_send, p_recv, o_send, o_recv,
):
    _, rows, dim = g_ref.shape
    quarter, half = dim // 4, dim // 2
    d = lax.axis_index("dp")
    s = lax.axis_index("shard")
    y, c = s // 2, lax.rem(s, 2)
    sib = 2 * y + 1 - c
    across = 2 * (1 - y) + c
    across_sib = 2 * (1 - y) + 1 - c

    def rows_of(index, size, count=None):
        return pl.ds(pl.multiple_of(index * size, size), count or size)

    def remote(src, dst, send, recv, device):
        return pltpu.make_async_remote_copy(
            src_ref=src, dst_ref=dst, send_sem=send, recv_sem=recv, device_id=device, device_id_type=MESH
        )

    g_in = pltpu.make_async_copy(g_ref, gin, local_sem.at[2])
    g_in.start()
    a_own = pltpu.make_async_copy(a_ref, abuf, local_sem.at[0])
    a_own.start()
    b_own = pltpu.make_async_copy(b_ref, bfull.at[rows_of(s, quarter)], local_sem.at[1])
    b_own.start()

    barrier = pltpu.get_barrier_semaphore()
    for k in range(1, groups):
        pl.semaphore_signal(barrier, inc=1, device_id=(flip(d, k), s), device_id_type=MESH)
    for other in (sib, across):
        pl.semaphore_signal(barrier, inc=1, device_id=(d, other), device_id_type=MESH)
    pl.semaphore_wait(barrier, groups + 1)

    own_half = rows_of(y, half)
    other_half = rows_of(1 - y, half)
    def layer_of(slot):
        found = 0
        for l in range(groups):
            found = jnp.where(owner_ref[l] == slot, l, found)
        return found

    parts = (s, sib, across, across_sib)
    order = (4, 2, 5, 3, 6, 1, 7)

    def gradient_copy(part, k):
        peer, columns = flip(d, k), rows_of(parts[part], quarter)
        return remote(
            gsend.at[k, :, columns], gbuf.at[rows_of(d, rows), columns],
            g_send.at[part, k], g_recv.at[part, k], (peer, s),
        )

    def arrival(part, k):
        peer, columns = flip(d, k), rows_of(parts[part], quarter)
        return remote(
            gsend.at[k, :, columns], gbuf.at[rows_of(peer, rows), columns],
            g_send.at[part, k], g_recv.at[part, k], (peer, s),
        )

    g_in.wait()
    for k in order:
        gsend[k] = gin[layer_of(flip(d, k))]
        gradient_copy(0, k).start()
    b_across = remote(
        b_ref.at[:, own_half], bfull.at[rows_of(s, quarter), own_half], b_send.at[0], b_recv.at[0], (d, across)
    )
    b_across.start()
    b_sib = remote(b_ref, bfull.at[rows_of(s, quarter)], b_send.at[1], b_recv.at[1], (d, sib))
    b_sib.start()
    a_sib = remote(a_ref.at[:, rows_of(across_sib, quarter)], asib, b_send.at[2], b_recv.at[2], (d, sib))
    a_sib.start()
    for part in range(1, 4):
        for k in order:
            gradient_copy(part, k).start()
    gbuf[rows_of(d, rows), :] = gin[layer_of(d)]

    a_own.wait()
    per = quarter // side

    def turn_own(i, carry):
        u, v = i // per, lax.rem(i, per)
        block = abuf[rows_of(u, side), pl.ds(pl.multiple_of(across * quarter + v * side, side), side)]
        ap[rows_of(v, side), pl.ds(pl.multiple_of(c * quarter + u * side, side), side)] = block.T
        return carry

    lax.fori_loop(0, per * per, turn_own, 0)
    a_sib.wait_recv()

    def turn_sib(i, carry):
        u, v = i // per, lax.rem(i, per)
        block = asib[rows_of(u, side), rows_of(v, side)]
        ap[rows_of(v, side), pl.ds(pl.multiple_of((1 - c) * quarter + u * side, side), side)] = block.T
        return carry

    lax.fori_loop(0, per * per, turn_sib, 0)

    b_own.wait()
    b_sib.wait_recv()
    wide = half // side

    def turn_b(i, carry):
        u, v = i // wide, lax.rem(i, wide)
        block = bfull[
            pl.ds(pl.multiple_of(y * half + u * side, side), side),
            pl.ds(pl.multiple_of((1 - y) * half + v * side, side), side),
        ]
        bfull[
            pl.ds(pl.multiple_of((1 - y) * half + v * side, side), side),
            pl.ds(pl.multiple_of(y * half + u * side, side), side),
        ] = block.T
        return carry

    lax.fori_loop(0, wide * wide, turn_b, 0)

    def add_part(part):
        for k in order:
            arrival(part, k).wait_recv()
        depth = rows_of(parts[part], quarter)

        def product(t, carry):
            columns = rows_of(t, tile)
            term = dot(gbuf[:, depth], bfull[depth, columns])
            if part == 0:
                acc[:, columns] = term
            elif part < 3:
                acc[:, columns] += term
            else:
                rbuf[here, columns] = (acc[:, columns] + term).astype(BF16)
                half_copy(t).start()
            return carry

        lax.fori_loop(0, dim // tile, product, 0)

    here = rows_of(c, quarter)

    def half_copy(t):
        block = rbuf.at[here, rows_of(t, tile)]
        return remote(block, block, r_send.at[t], r_recv.at[t], (d, sib))

    add_part(0)
    add_part(1)

    arrived = bfull.at[rows_of(across, quarter), other_half]
    remote(arrived, arrived, b_send.at[0], b_recv.at[0], (d, across)).wait_recv()
    relay = remote(arrived, arrived, b_send.at[3], b_recv.at[3], (d, sib))
    relay.start()
    add_part(2)
    relay.wait_recv()
    add_part(3)

    chunks = dim // width
    pieces = 2 * chunks
    z_half = d // (groups // 2)
    piece_rows = quarter // 2

    def place(i):
        late = lax.rem(i + c, 2)
        target = late * z_half + (1 - late) * (1 - z_half)
        return late, target, rows_of(target, piece_rows), rows_of(i // 2, width)

    def partial(i):
        return remote(psend.at[i], prec.at[i], p_send.at[i], p_recv.at[i], (d, across))

    per_tile = 2 * tile // width

    def give(i):
        _, _, here, columns = place(i)

        @pl.when(lax.rem(i, per_tile) == 0)
        def _():
            half_copy(i // per_tile).wait_recv()

        psend[i] = dot(ap[here, :], rbuf[:, columns]).astype(BF16)
        partial(i).start()

    def finish(i, carry):
        late, target, here, columns = place(i)
        mine = dot(abuf[here, own_half], rbuf[:, columns])
        partial(i).wait_recv()
        obuf[here, columns] = (mine + prec[i].astype(F32)).astype(BF16)
        for q in range(groups // 2):
            peer = target * (groups // 2) + lax.rem(flip(d, q), groups // 2)
            k = (1 - late) * (groups // 2) + q

            def send(peer=peer, k=k):
                remote(
                    obuf.at[rows_of(peer, rows), columns], o_ref.at[d, :, columns],
                    o_send.at[k], o_recv.at[k], (peer, s),
                ).start()

            if q == 0:
                pl.when(late == 0)(send)
            else:
                send()

        @pl.when(i + lead < pieces)
        def _():
            give(i + lead)

        return carry

    lead = 4
    for i in range(lead):
        give(i)
    lax.fori_loop(0, pieces, finish, 0)
    o_own = pltpu.make_async_copy(obuf.at[rows_of(d, rows)], o_ref.at[d], local_sem.at[3])
    o_own.start()

    for part in range(4):
        for k in order:
            gradient_copy(part, k).wait_send()
    for t in range(dim // tile):
        half_copy(t).wait_send()
    for copy in (b_across, b_sib, a_sib, relay):
        copy.wait_send()

    def sent(i, carry):
        partial(i).wait_send()
        return carry

    lax.fori_loop(0, pieces, sent, 0)
    o_own.wait()
    for k in range(1, groups):
        peer = flip(d, k)
        whole = remote(obuf.at[rows_of(peer, rows)], o_ref.at[peer], o_send.at[k], o_recv.at[k], (peer, s))
        whole.wait_send()
        whole.wait_recv()


def fused(gradient, owner, a_inverse, b_inverse):
    groups, rows, dim = gradient.shape
    quarter, half = dim // 4, dim // 2
    width, tile, side = 256, 256, 128
    chunks = dim // width
    anywhere = pl.BlockSpec(memory_space=pl.ANY)
    dma = pltpu.SemaphoreType.DMA
    returned = pl.pallas_call(
        functools.partial(kernel, groups, width, tile, side),
        out_shape=jax.ShapeDtypeStruct(gradient.shape, BF16),
        in_specs=[pl.BlockSpec(memory_space=pltpu.SMEM), anywhere, anywhere, anywhere],
        out_specs=anywhere,
        scratch_shapes=[
            pltpu.VMEM(gradient.shape, BF16),
            pltpu.VMEM(gradient.shape, BF16),
            pltpu.VMEM((quarter, dim), BF16),
            pltpu.VMEM((quarter, dim), F32),
            pltpu.VMEM((dim, dim), BF16),
            pltpu.VMEM((quarter, dim), BF16),
            pltpu.VMEM((quarter, quarter), BF16),
            pltpu.VMEM((quarter, half), BF16),
            pltpu.VMEM((half, dim), BF16),
            pltpu.VMEM((2 * chunks, quarter // 2, width), BF16),
            pltpu.VMEM((2 * chunks, quarter // 2, width), BF16),
            pltpu.VMEM((quarter, dim), BF16),
            dma((4,)),
            dma((4, groups)), dma((4, groups)),
            dma((4,)), dma((4,)),
            dma((dim // tile,)), dma((dim // tile,)),
            dma((2 * chunks,)), dma((2 * chunks,)),
            dma((groups,)), dma((groups,)),
        ],
        compiler_params=pltpu.CompilerParams(
            collective_id=0, has_side_effects=True, vmem_limit_bytes=60 * 1024 * 1024
        ),
        cost_estimate=pl.CostEstimate(
            flops=4 * quarter * dim * dim, bytes_accessed=8 * quarter * dim, transcendentals=0
        ),
    )(owner, gradient, a_inverse[0], b_inverse[0])
    return to_layers(owner, returned)


def solution(mesh):
    in_specs = (P(None, ("shard", "dp"), None), P(), P("dp", "shard", None), P("dp", "shard", None))
    out_specs = P(None, ("shard", "dp"), None)

    def program(gradient, owner, a_inverse, b_inverse):
        dim = gradient.shape[1]
        fits = mesh.shape["dp"] == 8 and mesh.shape["shard"] == 4 and dim % 512 == 0
        local = fused if fits and (dim // 32) % 16 == 0 else general
        return jax.shard_map(local, mesh=mesh, in_specs=in_specs, out_specs=out_specs, check_vma=False)(
            gradient, owner, a_inverse, b_inverse
        )

    return program
```

```python
import functools
import jax
import jax.numpy as jnp
from jax import lax
from jax.experimental import pallas as pl
from jax.experimental.pallas import tpu as pltpu
from jax.sharding import PartitionSpec as P

MESH = pl.DeviceIdType.MESH
F32 = jnp.float32
BF16 = jnp.bfloat16


def general(gradient, owner, a_inverse, b_inverse):
    layer_count = gradient.shape[0]
    chosen = (owner[:, None] == jnp.arange(layer_count, dtype=jnp.int32)[None, :]).astype(BF16)
    outgoing = jnp.einsum("lo,lrc->orc", chosen, gradient, preferred_element_type=F32).astype(BF16)
    owned = lax.all_to_all(outgoing, "dp", split_axis=0, concat_axis=1, tiled=True)
    right_half = jnp.dot(
        owned[0],
        lax.all_gather(b_inverse[0], "shard", axis=0, tiled=True),
        preferred_element_type=F32,
    ).astype(BF16)
    result_rows = jnp.dot(
        a_inverse[0],
        lax.all_gather(right_half, "shard", axis=0, tiled=True),
        preferred_element_type=F32,
    ).astype(BF16)
    returned = lax.all_to_all(
        result_rows[None, :, :], "dp", split_axis=1, concat_axis=0, tiled=True
    )
    return jnp.take(returned, owner, axis=0)


def collect(owner_ref, in_ref, out_ref, held, in_sems, out_sems):
    layers = in_ref.shape[0]
    loads = []
    for l in range(layers):
        loads.append(pltpu.make_async_copy(in_ref.at[owner_ref[l]], held.at[l], in_sems.at[l]))
        loads[-1].start()
    stores = []
    for l in range(layers):
        loads[l].wait()
        stores.append(pltpu.make_async_copy(held.at[l], out_ref.at[l], out_sems.at[l]))
        stores[-1].start()
    for store in stores:
        store.wait()


def to_layers(owner, array):
    layers, rows, dim = array.shape
    anywhere = pl.BlockSpec(memory_space=pl.ANY)
    return pl.pallas_call(
        collect,
        out_shape=jax.ShapeDtypeStruct(array.shape, array.dtype),
        in_specs=[pl.BlockSpec(memory_space=pltpu.SMEM), anywhere],
        out_specs=anywhere,
        scratch_shapes=[
            pltpu.VMEM(array.shape, array.dtype),
            pltpu.SemaphoreType.DMA((layers,)),
            pltpu.SemaphoreType.DMA((layers,)),
        ],
        cost_estimate=pl.CostEstimate(flops=0, bytes_accessed=4 * layers * rows * dim, transcendentals=0),
    )(owner, array)


def flip(index, mask):
    total, place = 0, 1
    while place <= mask:
        bit = lax.rem(index // place, 2)
        total = total + (1 - 2 * bit) * place if mask & place else total
        place *= 2
    return index + total


def dot(left, right):
    return jnp.dot(left, right, preferred_element_type=F32)


def kernel(
    groups, width, tile, side,
    owner_ref, g_ref, a_ref, b_ref, o_ref,
    gin, gsend, gbuf, acc, bfull, abuf, asib, ap, rbuf, psend, prec, obuf,
    local_sem, g_send, g_recv, b_send, b_recv, r_send, r_recv, p_send, p_recv, o_send, o_recv,
):
    _, rows, dim = g_ref.shape
    quarter, half = dim // 4, dim // 2
    d = lax.axis_index("dp")
    s = lax.axis_index("shard")
    y, c = s // 2, lax.rem(s, 2)
    sib = 2 * y + 1 - c
    across = 2 * (1 - y) + c
    across_sib = 2 * (1 - y) + 1 - c

    def rows_of(index, size, count=None):
        return pl.ds(pl.multiple_of(index * size, size), count or size)

    def remote(src, dst, send, recv, device):
        return pltpu.make_async_remote_copy(
            src_ref=src, dst_ref=dst, send_sem=send, recv_sem=recv, device_id=device, device_id_type=MESH
        )

    g_in = pltpu.make_async_copy(g_ref, gin, local_sem.at[2])
    g_in.start()
    a_own = pltpu.make_async_copy(a_ref, abuf, local_sem.at[0])
    a_own.start()
    b_own = pltpu.make_async_copy(b_ref, bfull.at[rows_of(s, quarter)], local_sem.at[1])
    b_own.start()

    barrier = pltpu.get_barrier_semaphore()
    for k in range(1, groups):
        pl.semaphore_signal(barrier, inc=1, device_id=(flip(d, k), s), device_id_type=MESH)
    for other in (sib, across):
        pl.semaphore_signal(barrier, inc=1, device_id=(d, other), device_id_type=MESH)
    pl.semaphore_wait(barrier, groups + 1)

    own_half = rows_of(y, half)
    other_half = rows_of(1 - y, half)
    def layer_of(slot):
        found = 0
        for l in range(groups):
            found = jnp.where(owner_ref[l] == slot, l, found)
        return found

    parts = (s, sib, across, across_sib)
    order = (4, 2, 5, 3, 6, 1, 7)

    def gradient_copy(part, k):
        peer, columns = flip(d, k), rows_of(parts[part], quarter)
        return remote(
            gsend.at[k, :, columns], gbuf.at[rows_of(d, rows), columns],
            g_send.at[part, k], g_recv.at[part, k], (peer, s),
        )

    def arrival(part, k):
        peer, columns = flip(d, k), rows_of(parts[part], quarter)
        return remote(
            gsend.at[k, :, columns], gbuf.at[rows_of(peer, rows), columns],
            g_send.at[part, k], g_recv.at[part, k], (peer, s),
        )

    g_in.wait()
    for k in order:
        gsend[k] = gin[layer_of(flip(d, k))]
        gradient_copy(0, k).start()
    b_across = remote(
        b_ref.at[:, own_half], bfull.at[rows_of(s, quarter), own_half], b_send.at[0], b_recv.at[0], (d, across)
    )
    b_across.start()
    b_sib = remote(b_ref, bfull.at[rows_of(s, quarter)], b_send.at[1], b_recv.at[1], (d, sib))
    b_sib.start()
    a_sib = remote(a_ref.at[:, rows_of(across_sib, quarter)], asib, b_send.at[2], b_recv.at[2], (d, sib))
    a_sib.start()
    for part in range(1, 4):
        for k in order:
            gradient_copy(part, k).start()
    gbuf[rows_of(d, rows), :] = gin[layer_of(d)]

    a_own.wait()
    per = quarter // side

    def turn_own(i, carry):
        u, v = i // per, lax.rem(i, per)
        block = abuf[rows_of(u, side), pl.ds(pl.multiple_of(across * quarter + v * side, side), side)]
        ap[rows_of(v, side), pl.ds(pl.multiple_of(c * quarter + u * side, side), side)] = block.T
        return carry

    lax.fori_loop(0, per * per, turn_own, 0)
    a_sib.wait_recv()

    def turn_sib(i, carry):
        u, v = i // per, lax.rem(i, per)
        block = asib[rows_of(u, side), rows_of(v, side)]
        ap[rows_of(v, side), pl.ds(pl.multiple_of((1 - c) * quarter + u * side, side), side)] = block.T
        return carry

    lax.fori_loop(0, per * per, turn_sib, 0)

    b_own.wait()
    b_sib.wait_recv()
    wide = half // side

    def turn_b(i, carry):
        u, v = i // wide, lax.rem(i, wide)
        block = bfull[
            pl.ds(pl.multiple_of(y * half + u * side, side), side),
            pl.ds(pl.multiple_of((1 - y) * half + v * side, side), side),
        ]
        bfull[
            pl.ds(pl.multiple_of((1 - y) * half + v * side, side), side),
            pl.ds(pl.multiple_of(y * half + u * side, side), side),
        ] = block.T
        return carry

    lax.fori_loop(0, wide * wide, turn_b, 0)

    def add_part(part, first=0, last=dim // tile):
        for k in order if first == 0 else ():
            arrival(part, k).wait_recv()
        depth = rows_of(parts[part], quarter)

        def product(t, carry):
            columns = rows_of(t, tile)
            term = dot(gbuf[:, depth], bfull[depth, columns])
            if part == 0:
                acc[:, columns] = term
            elif part < 3:
                acc[:, columns] += term
            else:
                rbuf[here, columns] = (acc[:, columns] + term).astype(BF16)
                half_copy(t).start()
            return carry

        lax.fori_loop(first, last, product, 0)

    here = rows_of(c, quarter)

    def half_copy(t):
        block = rbuf.at[here, rows_of(t, tile)]
        return remote(block, block, r_send.at[t], r_recv.at[t], (d, sib))

    add_part(0)
    add_part(1)

    arrived = bfull.at[rows_of(across, quarter), other_half]
    remote(arrived, arrived, b_send.at[0], b_recv.at[0], (d, across)).wait_recv()
    relay = remote(arrived, arrived, b_send.at[3], b_recv.at[3], (d, sib))
    relay.start()
    add_part(2)
    relay.wait_recv()
    early = 4
    add_part(3, 0, early)

    chunks = dim // width
    pieces = 2 * chunks
    z_half = d // (groups // 2)
    piece_rows = quarter // 2

    def place(i):
        late = lax.rem(i, 2)
        target = late * z_half + (1 - late) * (1 - z_half)
        return late, target, rows_of(target, piece_rows), rows_of(i // 2, width)

    def partial(i):
        return remote(psend.at[i], prec.at[i], p_send.at[i], p_recv.at[i], (d, across))

    per_tile = 2 * tile // width

    def give(i):
        _, _, here, columns = place(i)

        @pl.when(lax.rem(i, per_tile) == 0)
        def _():
            half_copy(i // per_tile).wait_recv()

        psend[i] = dot(ap[here, :], rbuf[:, columns]).astype(BF16)
        partial(i).start()

    def finish(i, carry):
        late, target, here, columns = place(i)
        mine = dot(abuf[here, own_half], rbuf[:, columns])
        partial(i).wait_recv()
        obuf[here, columns] = (mine + prec[i].astype(F32)).astype(BF16)
        for q in range(groups // 2):
            peer = target * (groups // 2) + lax.rem(flip(d, q), groups // 2)
            k = (1 - late) * (groups // 2) + q

            def send(peer=peer, k=k):
                remote(
                    obuf.at[rows_of(peer, rows), columns], o_ref.at[d, :, columns],
                    o_send.at[k], o_recv.at[k], (peer, s),
                ).start()

            if q == 0:
                pl.when(late == 0)(send)
            else:
                send()

        @pl.when(i + lead < pieces)
        def _():
            give(i + lead)

        return carry

    lead = 4
    for i in range(lead):
        give(i)
    add_part(3, early)
    lax.fori_loop(0, pieces, finish, 0)
    o_own = pltpu.make_async_copy(obuf.at[rows_of(d, rows)], o_ref.at[d], local_sem.at[3])
    o_own.start()

    for part in range(4):
        for k in order:
            gradient_copy(part, k).wait_send()
    for t in range(dim // tile):
        half_copy(t).wait_send()
    for copy in (b_across, b_sib, a_sib, relay):
        copy.wait_send()

    def sent(i, carry):
        partial(i).wait_send()
        return carry

    lax.fori_loop(0, pieces, sent, 0)
    o_own.wait()
    for k in range(1, groups):
        peer = flip(d, k)
        whole = remote(obuf.at[rows_of(peer, rows)], o_ref.at[peer], o_send.at[k], o_recv.at[k], (peer, s))
        whole.wait_send()
        whole.wait_recv()


def fused(gradient, owner, a_inverse, b_inverse):
    groups, rows, dim = gradient.shape
    quarter, half = dim // 4, dim // 2
    width, tile, side = 256, 256, 128
    chunks = dim // width
    anywhere = pl.BlockSpec(memory_space=pl.ANY)
    dma = pltpu.SemaphoreType.DMA
    returned = pl.pallas_call(
        functools.partial(kernel, groups, width, tile, side),
        out_shape=jax.ShapeDtypeStruct(gradient.shape, BF16),
        in_specs=[pl.BlockSpec(memory_space=pltpu.SMEM), anywhere, anywhere, anywhere],
        out_specs=anywhere,
        scratch_shapes=[
            pltpu.VMEM(gradient.shape, BF16),
            pltpu.VMEM(gradient.shape, BF16),
            pltpu.VMEM((quarter, dim), BF16),
            pltpu.VMEM((quarter, dim), F32),
            pltpu.VMEM((dim, dim), BF16),
            pltpu.VMEM((quarter, dim), BF16),
            pltpu.VMEM((quarter, quarter), BF16),
            pltpu.VMEM((quarter, half), BF16),
            pltpu.VMEM((half, dim), BF16),
            pltpu.VMEM((2 * chunks, quarter // 2, width), BF16),
            pltpu.VMEM((2 * chunks, quarter // 2, width), BF16),
            pltpu.VMEM((quarter, dim), BF16),
            dma((4,)),
            dma((4, groups)), dma((4, groups)),
            dma((4,)), dma((4,)),
            dma((dim // tile,)), dma((dim // tile,)),
            dma((2 * chunks,)), dma((2 * chunks,)),
            dma((groups,)), dma((groups,)),
        ],
        compiler_params=pltpu.CompilerParams(
            collective_id=0, has_side_effects=True, vmem_limit_bytes=60 * 1024 * 1024
        ),
        cost_estimate=pl.CostEstimate(
            flops=4 * quarter * dim * dim, bytes_accessed=8 * quarter * dim, transcendentals=0
        ),
    )(owner, gradient, a_inverse[0], b_inverse[0])
    return to_layers(owner, returned)


def solution(mesh):
    in_specs = (P(None, ("shard", "dp"), None), P(), P("dp", "shard", None), P("dp", "shard", None))
    out_specs = P(None, ("shard", "dp"), None)

    def program(gradient, owner, a_inverse, b_inverse):
        dim = gradient.shape[1]
        fits = mesh.shape["dp"] == 8 and mesh.shape["shard"] == 4 and dim % 512 == 0
        local = fused if fits and (dim // 32) % 16 == 0 else general
        return jax.shard_map(local, mesh=mesh, in_specs=in_specs, out_specs=out_specs, check_vma=False)(
            gradient, owner, a_inverse, b_inverse
        )

    return program
```
